512 devices in a mesh: seq: 16 (over x, y_hi, core), fsdp: 8 (over z), chan: 4 (over y_lo).
Axes of the slice: x: 4, y: 8 (y_hi: 2, y_lo: 4; y = y_hi * 4 + y_lo), z: 8, core: 2. Of those that a mesh axis runs over, the one named last changes fastest.
Arguments:
- tokens: bfloat16 [8192, 8192], P('seq', ('fsdp', 'chan')), may hold values from -600 to 600, as said below
- norm_gain: float32 [8192], replicated, may hold values from 0.1 to 1.9
- w_feat: bfloat16 [8192, 3, 4096], P('seq', None, ('fsdp', 'chan')), may hold values from -0.0625 to 0.0625
- pre_taps: float32 [3, 3, 4096], P(None, None, ('fsdp', 'chan')), may hold values from -2.5 to 2.5
- inner_taps: float32 [7, 4096], P(None, ('fsdp', 'chan')), may hold values from -2.5 to 2.5
- w_out: bfloat16 [4096, 8192], P('seq', ('fsdp', 'chan')), may hold values from -0.09375 to 0.09375
Outputs:
- mixed: bfloat16 [8192, 8192], P('seq', ('fsdp', 'chan'))
The draws below stay inside these ranges and needn't reach their ends.
Inputs may be any that keep to these rules, and one draw needn't show every extreme that they name: `tokens`: finite activations.
All inputs are finite; a program needn't handle non-finite values.
Results may differ from the reference program's by a relative error of at most 0.0085.
Values may be sent and summed in bfloat16 or wider, within the bound.
A program may use at most 64 MiB of HBM per device.

```python
import math
import jax
import jax.numpy as jnp
from jax import lax

D = 8192
C = 4096
TOKENS = 8192


def draw_tokens(key, part):
    key = jax.random.fold_in(key, 11)
    key_rows, key_cols, key_main = jax.random.split(key, 3)
    col_scale = jnp.exp(jax.random.uniform(key_cols, (1, D), jnp.float32, 0.0, math.log(10.0)))
    row_scale = jnp.exp(jax.random.uniform(key_rows, (TOKENS, 1), jnp.float32, 0.0, math.log(10.0)))
    values = jnp.clip(jax.random.normal(key_main, (TOKENS, D), jnp.float32), -4.0, 4.0)
    values = values * row_scale * col_scale
    return values.astype(jnp.bfloat16)


def steps_of(stream_key, dims, shards, least, largest):
    def one(position, blocks):
        heights = jax.random.uniform(jax.random.fold_in(jax.random.fold_in(stream_key, 6), position), (blocks,), jnp.float32, least / len(shards), largest / len(shards))
        return jnp.repeat(jnp.exp(heights), dims[position] // blocks).reshape((-1,) + (1,) * (len(dims) - position - 1))

    factor_of = one(*shards[0])
    for cut in shards[1:]:
        factor_of = factor_of * one(*cut)
    return factor_of


def gaussian(own_key, shape, scale, most, cuts=(), kind=jnp.bfloat16):
    level = steps_of(own_key, shape, cuts, -0.22, 0.18) if cuts else 1.0
    drawn = jax.random.normal(own_key, shape, jnp.float32) * scale * level
    return jnp.minimum(jnp.maximum(drawn, -most), most).astype(kind)


def setup_inputs(seed: int = 0) -> dict:
    key_of = jax.random.split(jax.random.key(seed), 7)
    return {
        "tokens": draw_tokens(jax.random.fold_in(key_of[6], 71), 0),
        "norm_gain": jnp.clip(1.0 + 0.18 * jax.random.normal(key_of[1], (D,), jnp.float32), 0.1, 1.9),
        "w_feat": gaussian(key_of[2], (D, 3, C), D ** -0.5, 0.0625, ((0, 16), (2, 32))),
        "pre_taps": gaussian(key_of[3], (3, 3, C), 0.6, 2.5, ((2, 32),), jnp.float32),
        "inner_taps": gaussian(key_of[4], (7, C), 0.4, 2.5, ((1, 32),), jnp.float32),
        "w_out": gaussian(key_of[5], (C, D), C ** -0.5, 0.09375, ((0, 16), (1, 32))),
    }


def short_conv(extended, tap_table, length_out):
    width_taps = tap_table.shape[0]
    result = jnp.zeros((length_out,) + extended.shape[1:], jnp.float32)
    for lag in range(width_taps):
        begin = width_taps - 1 - lag
        result = result + tap_table[lag] * extended[begin:begin + length_out].astype(jnp.float32)
    return result

def reference(tokens, norm_gain, w_feat, pre_taps, inner_taps, w_out):
    widened = tokens.astype(jnp.float32)
    row_scale = lax.rsqrt(lax.optimization_barrier(jnp.mean(widened * widened, axis=1, keepdims=True)) + 1e-06)
    normed = (widened * row_scale * norm_gain).astype(jnp.bfloat16)
    features = jnp.dot(normed, w_feat.reshape(D, 3 * C), preferred_element_type=jnp.float32)
    features = features.astype(jnp.bfloat16).reshape(TOKENS, 3, C)
    padded = jnp.concatenate([jnp.zeros((2, 3, C), features.dtype), features], axis=0)
    filtered = short_conv(padded, pre_taps, TOKENS)
    key_value = filtered[:, 1] * filtered[:, 2]
    padded_kv = jnp.concatenate([jnp.zeros((6, C), jnp.float32), key_value], axis=0)
    inner_out = short_conv(padded_kv, inner_taps, TOKENS)
    gated = (filtered[:, 0] * inner_out).astype(jnp.bfloat16)
    return jnp.dot(gated, w_out, preferred_element_type=jnp.float32).astype(jnp.bfloat16)
```

```python
import heapq

import jax
import jax.numpy as jnp
from jax import lax
from jax.experimental import pallas as pl
from jax.experimental.pallas import tpu as pltpu
from jax.sharding import PartitionSpec as P

MESH = pl.DeviceIdType.MESH
F32, BF16 = jnp.float32, jnp.bfloat16
SLAB, HALO, EXT = 512, 16, 528
NSEM = 160
TOKEN_ROWS = ((272, 256), (0, 272))
GATED_ROWS = ((272, 240), (0, 272))


def body(
    tok, gain, wf, pre, inner, wo, out,
    xr, xn, panel, panel_out, acc, psend, precv, feats, kv, ssq, ssend, srecv, gat, acc2, osend, orecv,
    send_sem, recv_sem, local_sem,
):
    s, z, c = lax.axis_index("seq"), lax.axis_index("fsdp"), lax.axis_index("chan")
    kappa = lax.rem(c, 2)
    high = c // 2
    c1 = c + 1 - 2 * kappa
    c2 = lax.rem(c + 2, 4)
    core = lax.rem(s, 2)
    y_hi = lax.rem(s // 2, 2)
    zp, zm = lax.rem(z + 1, 8), lax.rem(z + 7, 8)
    dev_zp, dev_zm = (s, zp, c), (s, zm, c)
    dev_c1, dev_c2 = (s, z, c1), (s, z, c2)
    s_yh = s + 2 - 4 * y_hi
    dev_yh = (s_yh, z, c)
    dev_xp, dev_xm = (lax.rem(s + 4, 16), z, c), (lax.rem(s + 12, 16), z, c)
    s_sib = s + 1 - 2 * core
    dev_sib = (s_sib, z, c)
    dev_next, dev_prev = (lax.rem(s + 1, 16), z, c), (lax.rem(s + 15, 16), z, c)
    peers = (dev_zp, dev_zm, dev_c1, dev_c2, dev_yh, dev_xp, dev_xm, dev_sib, dev_next, dev_prev)

    barrier = pltpu.get_barrier_semaphore()
    for dev in peers:
        pl.semaphore_signal(barrier, inc=1, device_id=dev, device_id_type=MESH)
    pl.semaphore_wait(barrier, len(peers))

    started, count = [], [0]

    def send(src, dst, dev):
        k = count[0]
        count[0] += 1
        copy = pltpu.make_async_remote_copy(src, dst, send_sem.at[k], recv_sem.at[k], device_id=dev, device_id_type=MESH)
        copy.start()
        started.append(copy)
        return k

    def arrived(k, landed):
        pltpu.make_async_remote_copy(
            landed, landed, send_sem.at[k], recv_sem.at[k], device_id=dev_zp, device_id_type=MESH
        ).wait_recv()

    def block_of(steps, hi):
        return 2 * lax.rem(z + steps + 8, 8) + hi

    done = {}

    def ring(view, begin, hop, key, own_hi, far_right):
        own = view(block_of(0, own_hi))
        right = send(own, own, dev_zp)
        left = send(own, own, dev_zm)
        for step in (1, 2, 3, 4):
            yield begin + hop * step
            take_right = step < 4 or far_right
            take_left = step < 4 or not far_right
            if take_right:
                landed = view(block_of(-step, own_hi))
                arrived(right, landed)
                if step < 3 or (step == 3 and far_right):
                    right = send(landed, landed, dev_zp)
            if take_left:
                landed = view(block_of(step, own_hi))
                arrived(left, landed)
                if step < 3 or (step == 3 and not far_right):
                    left = send(landed, landed, dev_zm)
        done[key] = True

    def gather(view, begin, hop, other, key):
        mine = view(block_of(0, high))
        k = send(mine, mine, dev_c2)
        first = ring(view, begin, hop, key + ("a",), high, True)
        t_first = next(first)
        t_other = begin + other
        second = None
        while first is not None or second is not None or t_other is not None:
            options = [t for t in (t_first, t_other) if t is not None]
            if second is not None:
                options.append(t_second)
            now = min(options)
            yield now
            if t_other is not None and now == t_other:
                arrived(k, view(block_of(0, 1 - high)))
                second = ring(view, now, hop, key + ("b",), 1 - high, False)
                t_second = next(second)
                t_other = None
            elif first is not None and now == t_first:
                t_first = next(first, None)
                if t_first is None:
                    first = None
            else:
                t_second = next(second, None)
                if t_second is None:
                    second = None
        done[key] = True

    def weights(src, dst, rows, cols, begin, scale, key):
        def place(block, part):
            return dst.at[pl.ds(pl.multiple_of(block * rows, rows), rows), pl.ds(part * cols, cols)]

        def whole(block):
            return dst.at[pl.ds(pl.multiple_of(block * rows, rows), rows), :]

        swap = send(src.at[pl.ds(pl.multiple_of((1 - kappa) * rows, rows), rows), :], place(s, 1), dev_c1)
        held = src.at[pl.ds(pl.multiple_of(kappa * rows, rows), rows), :]
        local = pltpu.make_async_copy(held, place(s, 0), local_sem.at[0 if key == "w" else 1])
        local.start()
        far = [send(held, place(s, 0), dev_yh)]
        chains = []

        def chain(block, part, src_ref, at):
            right = send(src_ref, place(block, part), dev_xp)
            left = send(src_ref, place(block, part), dev_xm)
            yield at + 8 * scale
            landed = place(lax.rem(block + 12, 16), part)
            arrived(right, landed)
            if part == 0:
                last = send(landed, landed, dev_xp)
            landed = place(lax.rem(block + 4, 16), part)
            arrived(left, landed)
            if part == 1:
                last = send(landed, landed, dev_xm)
            yield at + 16 * scale
            arrived(last, place(lax.rem(block + 8, 16), part))

        order = 0

        def add(gen):
            nonlocal order
            t = next(gen, None)
            if t is not None:
                heapq.heappush(chains, (t, order, gen))
                order += 1

        def swapped():
            yield begin + 6 * scale
            arrived(swap, place(s, 1))
            far.append(send(place(s, 1), place(s, 1), dev_yh))
            add(chain(s, 1, place(s, 1), begin + 6 * scale))
            yield begin + 14 * scale
            arrived(far[0], place(s_yh, 0))
            add(chain(s_yh, 0, place(s_yh, 0), begin + 14 * scale))
            yield begin + 24 * scale
            arrived(far[1], place(s_yh, 1))
            add(chain(s_yh, 1, place(s_yh, 1), begin + 24 * scale))

        add(chain(s, 0, held, begin))
        add(swapped())
        while chains:
            t, _, gen = heapq.heappop(chains)
            yield t
            add(gen)
        local.wait()
        mine, copies = [], []
        for i in range(8):
            block = 2 * i + core
            copies.append(send(whole(block), whole(block), dev_sib))
        yield begin + 42 * scale
        for i, k in enumerate(copies):
            arrived(k, whole(2 * i + 1 - core))
        done[key] = True

    def needs(*keys):
        return all(key in done for key in keys)

    def scaled(chunk):
        r0, nr = TOKEN_ROWS[chunk]
        gains = [gain[:, pl.ds(pl.multiple_of(b * 512 + kappa * 256, 256), 256)] for b in range(16)]

        @pl.loop(0, nr // 16)
        def _(i):
            rows = pl.ds(pl.multiple_of(r0 + i * 16, 16), 16)
            total = jnp.zeros((16, 128), F32)
            for b in range(16):
                x = xr[b, rows, :].astype(F32)
                total = total + x[:, :128] * x[:, :128] + x[:, 128:] * x[:, 128:]
                xn[rows, b * 256 : (b + 1) * 256] = (x * gains[b]).astype(BF16)
            ssq[rows, :] = total

    def squares(chunk):
        r0, nr = TOKEN_ROWS[chunk]
        part = lax.dot_general(
            jnp.ones((8, 128), F32), ssq[r0 : r0 + nr, :], (((1,), (1,)), ((), ())),
            precision=lax.Precision.HIGHEST, preferred_element_type=F32,
        )
        ssend[chunk, :, 0:nr] = part

    def product(chunk, half):
        r0, nr = TOKEN_ROWS[chunk]
        cols = slice(half * 384, half * 384 + 384)
        acc[r0 : r0 + nr, :] = jnp.dot(xn[r0 : r0 + nr, 0:1024], panel[0:1024, cols], preferred_element_type=F32)

        @pl.loop(1, 4)
        def _(k):
            depth = pl.ds(pl.multiple_of(k * 1024, 1024), 1024)
            acc[r0 : r0 + nr, :] += jnp.dot(xn[r0 : r0 + nr, depth], panel[depth, cols], preferred_element_type=F32)

    def combine(chunk):
        r0, nr = TOKEN_ROWS[chunk]
        both = ssend[chunk, :, 0:nr] + srecv[chunk, :, 0:nr]
        eye = (lax.broadcasted_iota(jnp.int32, (nr, nr), 0) == lax.broadcasted_iota(jnp.int32, (nr, nr), 1)).astype(F32)
        column = lax.dot_general(
            eye, both, (((1,), (1,)), ((), ())), precision=lax.Precision.HIGHEST, preferred_element_type=F32
        )[:, 0:1]
        scale = lax.rsqrt(column * (1.0 / 8192.0) + 1e-06)
        if chunk == 1:
            row = lax.broadcasted_iota(jnp.int32, (nr, 1), 0)
            scale = jnp.where((row < HALO) & (s == 0), 0.0, scale)
        total = acc[r0 : r0 + nr, :] + precv[r0 : r0 + nr, :].astype(F32)
        feats[r0 : r0 + nr, :] = total * scale

    def gates(chunk):
        t0, nr = GATED_ROWS[chunk]
        e0 = t0 + HALO

        def filtered(i, begin, rows):
            value = jnp.zeros((rows, 128), F32)
            for lag in range(3):
                value = value + pre[lag, i : i + 1, :] * feats[begin - lag : begin - lag + rows, i * 128 : i * 128 + 128]
            return value

        kv[e0 - 8 : e0 + nr, :] = filtered(1, e0 - 8, nr + 8) * filtered(2, e0 - 8, nr + 8)
        value = jnp.zeros((nr, 128), F32)
        for lag in range(7):
            value = value + inner[lag : lag + 1, :] * kv[e0 - lag : e0 - lag + nr, :]
        block = pl.multiple_of((2 * z + high) * 128, 128)
        gat[t0 : t0 + nr, pl.ds(block, 128)] = (filtered(0, e0, nr) * value).astype(BF16)

    def product_out(chunk):
        t0, nr = GATED_ROWS[chunk]
        acc2[t0 : t0 + nr, :] = jnp.dot(gat[t0 : t0 + nr, 0:1024], panel_out[0:1024, :], preferred_element_type=F32)
        acc2[t0 : t0 + nr, :] += jnp.dot(gat[t0 : t0 + nr, 1024:2048], panel_out[1024:2048, :], preferred_element_type=F32)

    def x_view(chunk):
        r0, nr = TOKEN_ROWS[chunk]
        return lambda block: xr.at[block, pl.ds(r0, nr), :]

    def g_view(chunk):
        t0, nr = GATED_ROWS[chunk]
        return lambda block: gat.at[pl.ds(t0, nr), pl.ds(pl.multiple_of(block * 128, 128), 128)]

    ssend[...] = jnp.zeros_like(ssend)
    mine = block_of(0, high)
    xr[mine, HALO:EXT, :] = tok[...]
    halo_k = send(tok.at[pl.ds(SLAB - HALO, HALO), :], xr.at[mine, pl.ds(0, HALO), :], dev_next)

    def stage_one(chunk, begin, compute_at):
        if chunk == 1:
            yield begin
            arrived(halo_k, xr.at[mine, pl.ds(0, HALO), :])
        yield from gather(x_view(chunk), begin, 5.5, 8, ("x", chunk))
        yield compute_at
        scaled(chunk)
        squares(chunk)
        while "w" not in done:
            yield compute_at
            compute_at += 1
        yield compute_at
        r0, nr = TOKEN_ROWS[chunk]
        product(chunk, 1)
        psend[r0 : r0 + nr, :] = acc[r0 : r0 + nr, :].astype(BF16)
        k1 = send(psend.at[pl.ds(r0, nr), :], precv.at[pl.ds(r0, nr), :], dev_c1)
        k2 = send(ssend.at[chunk], srecv.at[chunk], dev_c1)
        yield compute_at + 2
        product(chunk, 0)
        yield compute_at + 6
        arrived(k1, precv.at[pl.ds(r0, nr), :])
        arrived(k2, srecv.at[chunk])
        combine(chunk)
        gates(chunk)
        at = compute_at + 8
        yield from gather(g_view(chunk), at, 2.6, 4, ("g", chunk))
        yield at + 14
        while "wo" not in done:
            at += 1
            yield at
        product_out(chunk)
        t0, ng = GATED_ROWS[chunk]
        osend[t0 : t0 + ng, :] = acc2[t0 : t0 + ng, 256:512].astype(BF16)
        k3 = send(osend.at[pl.ds(t0, ng), :], orecv.at[pl.ds(t0, ng), :], dev_c1)
        yield at + 19
        arrived(k3, orecv.at[pl.ds(t0, ng), :])
        out[t0 : t0 + ng, :] = (acc2[t0 : t0 + ng, 0:256] + orecv[t0 : t0 + ng, :].astype(F32)).astype(BF16)

    streams = []
    gens = [
        (0, stage_one(0, 0, 28)),
        (0.1, weights(wf, panel, 256, 384, 0, 1.0, "w")),
        (3, stage_one(1, 6, 45)),
        (20, weights(wo, panel_out, 128, 256, 20, 0.6, "wo")),
    ]
    for i, (t, gen) in enumerate(gens):
        heapq.heappush(streams, (t, i, gen))
    while streams:
        _, i, gen = heapq.heappop(streams)
        t = next(gen, None)
        if t is not None:
            heapq.heappush(streams, (t, i, gen))
    for copy in started:
        copy.wait_send()


def on_device(tokens, norm_gain, w_feat, pre_taps, inner_taps, w_out):
    vmem = pl.BlockSpec(memory_space=pltpu.VMEM)
    return pl.pallas_call(
        body,
        out_shape=jax.ShapeDtypeStruct((SLAB, 256), BF16),
        in_specs=[vmem] * 6,
        out_specs=vmem,
        scratch_shapes=[
            pltpu.VMEM((16, EXT, 256), BF16),
            pltpu.VMEM((EXT, 4096), BF16),
            pltpu.VMEM((4096, 768), BF16),
            pltpu.VMEM((2048, 512), BF16),
            pltpu.VMEM((EXT, 384), F32),
            pltpu.VMEM((EXT, 384), BF16),
            pltpu.VMEM((EXT, 384), BF16),
            pltpu.VMEM((EXT, 384), F32),
            pltpu.VMEM((EXT, 128), F32),
            pltpu.VMEM((EXT, 128), F32),
            pltpu.VMEM((2, 8, 384), F32),
            pltpu.VMEM((2, 8, 384), F32),
            pltpu.VMEM((SLAB, 2048), BF16),
            pltpu.VMEM((SLAB, 512), F32),
            pltpu.VMEM((SLAB, 256), BF16),
            pltpu.VMEM((SLAB, 256), BF16),
            pltpu.SemaphoreType.DMA((NSEM,)),
            pltpu.SemaphoreType.DMA((NSEM,)),
            pltpu.SemaphoreType.DMA((2,)),
        ],
        compiler_params=pltpu.CompilerParams(
            collective_id=0, has_side_effects=True, vmem_limit_bytes=56 * 1024 * 1024
        ),
    )(tokens, norm_gain.reshape(1, 8192), w_feat.reshape(512, 384), pre_taps, inner_taps, w_out)


def solution(mesh):
    in_specs = (
        P("seq", ("fsdp", "chan")),
        P(),
        P("seq", None, ("fsdp", "chan")),
        P(None, None, ("fsdp", "chan")),
        P(None, ("fsdp", "chan")),
        P("seq", ("fsdp", "chan")),
    )
    out_specs = P("seq", ("fsdp", "chan"))
    return jax.shard_map(
        on_device, mesh=mesh, in_specs=in_specs, out_specs=out_specs, check_vma=False
    )
```

```python
import jax
import jax.numpy as jnp
from jax import lax
from jax.experimental import pallas as pl
from jax.experimental.pallas import tpu as pltpu
from jax.sharding import PartitionSpec as P

MESH = pl.DeviceIdType.MESH
F32, BF16 = jnp.float32, jnp.bfloat16
SLAB, HALO, EXT = 512, 16, 528
N_SEND, N_RECV = 40, 211
TOKEN_ROWS = ((384, 512), (256, 384), (128, 256), (0, 128))
CHUNKS = ((384, 512), (256, 384), (128, 256), (0, 128))
RATE = {"z+": 45.0, "z-": 45.0, "x+": 45.0, "x-": 45.0, "y": 22.5, "c1": 45.0, "core": 400.0}
LATENCY = 2.8
FAIR = ("y", "c1")
TOKEN_BEGIN = (0.0, 1.6, 5.3, 26.8)
RIGHT, LEFT = {(1, 0): [(2, 0)], (2, 0): [(3, 0)], (3, 0): [(4, 0)]}, {(-1, 0): [(-2, 0)], (-2, 0): [(-3, 0)]}
OTHER = {(1, 1): [(2, 1)], (2, 1): [(3, 1)], (-1, 1): [(-2, 1)], (-2, 1): [(-3, 1)], (-3, 1): [(-4, 1)]}
SKIP = {
    (1, 0): [(3, 0), (2, 0)], (3, 0): [(4, 0)], (-1, 0): [(-2, 0)], (-2, 0): [(-3, 0)],
    (1, 1): [(2, 1)], (2, 1): [(3, 1)], (-1, 1): [(-3, 1), (-2, 1)], (-3, 1): [(-4, 1)],
}
OTHER_Y = {(1, 1): [(2, 1)], (2, 1): [(3, 1)], (-1, 1): [(-2, 1)], (-2, 1): [(-3, 1)], (4, 0): [(4, 1)]}
TREES = {
    "ring": {(0, 0): [(0, 1), (1, 0), (-1, 0)], (0, 1): [(-1, 1), (1, 1)], **RIGHT, **LEFT, **OTHER},
    "diag": {(0, 0): [(1, 0), (-1, 0), (-1, 1), (1, 1), (0, 1)], **RIGHT, **LEFT, **OTHER},
    "skip": {(0, 0): [(0, 1), (1, 0), (-1, 0)], (0, 1): [(-1, 1), (1, 1)], **SKIP},
    "fast": {(0, 0): [(1, 0), (-1, 1), (-1, 0), (1, 1), (0, 1)], **SKIP},
    "viay": {(0, 0): [(0, 1), (1, 0), (-1, 0)], (0, 1): [(-1, 1), (1, 1)], **RIGHT, **LEFT, **OTHER_Y},
}
TOKEN_TREE = ("ring", "viay", "ring", "skip")
GATED_TREE = ("ring", "diag", "viay", "fast")
WO_BEGIN = 33.0
FAR_AFTER = True
FAR_SPLIT = 2
FAR_DIRECT = True


class Plan:
    def __init__(self):
        self.clock, self.flows, self.landed, self.left = 0.0, [], {}, {}
        self.flags, self.streams, self.order, self.log = set(), [], 0, []

    def spawn(self, gen, rank=0):
        self.order += 1
        self.resume([rank, self.order, gen, None])

    def resume(self, stream):
        stream[3] = next(stream[2], None)
        if stream[3] is not None:
            self.streams.append(stream)

    def start(self, key, link, kib):
        if key is None:
            self.order += 1
            key = -self.order
        self.flows.append([key, link, float(kib)])
        self.clock_to(self.clock + 0.08)

    def busy(self, us):
        self.clock_to(self.clock + us)

    def shares(self):
        total = {}
        for flow in self.flows:
            total.setdefault(flow[1], []).append(flow)
        share = {}
        for link, flows in total.items():
            for i, flow in enumerate(flows):
                share[flow[0]] = RATE[link] / len(flows) if link in FAIR else RATE[link] * (i == 0)
        return share

    def clock_to(self, until):
        while True:
            share = self.shares()
            ends = [flow[2] / share[flow[0]] for flow in self.flows if share[flow[0]]]
            step = min(ends + [until - self.clock])
            for flow in self.flows:
                flow[2] -= step * share[flow[0]]
            self.clock += step
            for flow in [f for f in self.flows if f[2] <= 1e-6]:
                self.flows.remove(flow)
                self.left[flow[0]] = self.clock + 0.3
                self.landed[flow[0]] = self.clock + LATENCY
            if self.clock >= until - 1e-9:
                return

    def when(self, need):
        if isinstance(need, float):
            return need
        if isinstance(need, str):
            return 0.0 if need in self.flags else None
        if isinstance(need, tuple):
            return self.left.get(need[1])
        return self.landed.get(need)

    def run(self):
        while self.streams:
            best = None
            for stream in self.streams:
                times = [self.when(need) for need in stream[3]]
                if any(t is None for t in times):
                    continue
                at = max(times + [0.0])
                ready = (max(at, self.clock), stream[0], at, stream[1])
                if best is None or ready < best[0]:
                    best = (ready, stream)
            share = self.shares()
            ends = [self.clock + flow[2] / share[flow[0]] for flow in self.flows if share[flow[0]]]
            if best is not None and (not ends or best[0][0] <= min(ends)):
                self.clock_to(max(best[0][0], self.clock))
                self.streams.remove(best[1])
                self.resume(best[1])
            else:
                self.clock_to(min(ends))


def body(
    tok_hbm, gain_hbm, w3, pre_hbm, inner_hbm, wo_hbm, out_hbm,
    gain, pre, inner, wo, out, wf, xr, xn, panel, panel_out, acc, psend, precv, feats, edge, kv, ssq, ssend, srecv, gat, acc2, osend, orecv,
    send_sem, recv_sem, local_sem, load_sem, store_sem,
):
    s, z, c = lax.axis_index("seq"), lax.axis_index("fsdp"), lax.axis_index("chan")
    kappa = lax.rem(c, 2)
    high = c // 2
    c1 = c + 1 - 2 * kappa
    c2 = lax.rem(c + 2, 4)
    core = lax.rem(s, 2)
    y_hi = lax.rem(s // 2, 2)
    s_yh = s + 2 - 4 * y_hi
    s_sib = s + 1 - 2 * core
    zp, zm = (s, lax.rem(z + 1, 8), c), (s, lax.rem(z + 7, 8), c)
    dev_c1, dev_c2 = (s, z, c1), (s, z, c2)
    dev_yh, dev_yh1 = (s_yh, z, c), (s_yh, z, c1)
    xp, xm = (lax.rem(s + 4, 16), z, c), (lax.rem(s + 12, 16), z, c)
    xf = (lax.rem(s + 8, 16), z, c)
    dev_sib = (s_sib, z, c)
    dev_next, dev_prev = (lax.rem(s + 1, 16), z, c), (lax.rem(s + 15, 16), z, c)
    peers = (zp, zm, dev_c1, dev_c2, dev_yh, dev_yh1, xp, xm, xf, dev_sib, dev_next, dev_prev)

    barrier = pltpu.get_barrier_semaphore()
    for dev in peers:
        pl.semaphore_signal(barrier, inc=1, device_id=dev, device_id_type=MESH)
    loads = [
        pltpu.make_async_copy(src, dst, load_sem.at[i])
        for i, (src, dst) in enumerate(
            [(tok_hbm, xr.at[2 * z + high])]
            + [(w3.at[i], wf.at[:, pl.ds(i * 128, 128)]) for i in range(3)]
            + [(wo_hbm, wo), (gain_hbm, gain), (pre_hbm, pre), (inner_hbm, inner)]
        )
    ]
    for load in loads:
        load.start()
    feats[0:8, :] = jnp.zeros((8, 384), F32)
    ssend[...] = jnp.zeros_like(ssend)
    pl.semaphore_wait(barrier, len(peers))
    for load in loads:
        load.wait()

    plan = Plan()
    started, flying = [], []

    def send(src, dst, dev, link, kib):
        k = len(started)
        if len(flying) < N_SEND:
            slot = len(flying)
        else:
            old, slot = flying.pop(0)
            sent(old)
        copy = pltpu.make_async_remote_copy(src, dst, send_sem.at[slot], recv_sem.at[k], device_id=dev, device_id_type=MESH)
        copy.start()
        started.append([copy, False])
        flying.append((k, slot))
        plan.start(k, link, kib)
        return k

    def sent(k):
        if not started[k][1]:
            started[k][0].wait_send()
            started[k][1] = True

    def arrived(k, landed):
        pltpu.make_async_remote_copy(
            landed, landed, send_sem.at[0], recv_sem.at[k], device_id=zp, device_id_type=MESH
        ).wait_recv()

    def block_of(steps, hi):
        return 2 * lax.rem(z + steps + 8, 8) + hi

    def gather(view, kib, use, flag, tree):
        count = [0]

        def holder(node):
            return block_of(-node[0], high if node[1] == 0 else 1 - high)

        def pass_on(node):
            ref = view(holder(node))
            for child in tree.get(node, ()):
                steps, turn = child[0] - node[0], child[1] != node[1]
                dev = (s, lax.rem(z + steps + 8, 8), c2 if turn else c)
                link = "z+" if steps > 0 else "z-"
                if turn and steps:
                    plan.start(None, link, kib)
                k = send(ref, ref, dev, "y" if turn else link, kib * (1 if turn else abs(steps)))
                plan.spawn(take(child, k))
            use(holder(node))
            count[0] += 1
            if count[0] == 16:
                plan.flags.add(flag)

        def take(node, k):
            yield [k]
            arrived(k, view(holder(node)))
            pass_on(node)

        pass_on((0, 0))

    def weights(src, dst, rows, cols, key, sem):
        def place(block, piece):
            part, r0, nr = piece
            return dst.at[pl.ds(pl.multiple_of(block * rows + r0, 16), nr), pl.ds(part * cols, cols)]

        def mine(piece):
            part, r0, nr = piece
            half = kappa if part == 0 else 1 - kappa
            return src.at[pl.ds(pl.multiple_of(half * rows + r0, 16), nr), :]

        def kib(piece):
            return piece[2] * cols * 2 / 1024

        rest = [2 * 16 * rows]
        local = pltpu.make_async_copy(mine((0, 0, rows)), place(s, (0, 0, rows)), sem)

        def to_sibling(base, far, piece, ref):
            k = send(ref, place(lax.rem(base + far, 16), piece), dev_sib, "core", kib(piece))

            def take():
                yield [k]
                arrived(k, place(lax.rem(base + 1 - 2 * core + far, 16), piece))
                rest[0] -= 2 * piece[2]
                if not rest[0]:
                    local.wait()
                    plan.flags.add(key)

            plan.spawn(take(), 1)

        def across(base, piece, ref, direct):
            part = piece[0]
            kr = send(ref, place(base, piece), xp, "x+", kib(piece))
            kl = send(ref, place(base, piece), xm, "x-", kib(piece))
            if direct:
                plan.start(None, "x-", kib(piece))
                kf = send(ref, place(base, piece), xf, "x+", kib(piece))

            def take(k, far, onward, dev, link):
                yield [k]
                ref = place(lax.rem(base + far, 16), piece)
                arrived(k, ref)
                if onward:
                    k = send(ref, ref, dev, link, kib(piece))
                to_sibling(base, far, piece, ref)
                if onward:
                    yield [k]
                    ref = place(lax.rem(base + 8, 16), piece)
                    arrived(k, ref)
                    to_sibling(base, 8, piece, ref)

            plan.spawn(take(kr, 12, part == 0 and not direct, xp, "x+"))
            plan.spawn(take(kl, 4, part == 1 and not direct, xm, "x-"))
            if direct:
                plan.spawn(take(kf, 8, False, None, None))
            to_sibling(base, 0, piece, ref)

        def far(k, piece, direct):
            yield [k]
            arrived(k, place(s_yh, piece))
            across(s_yh, piece, place(s_yh, piece), direct)

        def far_piece(piece, direct):
            k = send(mine(piece), place(s, piece), dev_yh if piece[0] == 0 else dev_yh1, "y", kib(piece))
            plan.spawn(far(k, piece, direct))
            return k

        def swapped():
            yield [swap]
            arrived(swap, place(s, (1, 0, rows)))
            across(s, (1, 0, rows), place(s, (1, 0, rows)), False)

        def later(pieces, k):
            for i, piece in enumerate(pieces):
                if FAR_AFTER:
                    yield [("sent", k)]
                    sent(k)
                k = far_piece(piece, FAR_DIRECT and i == len(pieces) - 1)
            yield [0.0]

        n = rows // FAR_SPLIT if key == "w" else rows
        pieces = [(part, r0, n) for part in (0, 1) for r0 in range(0, rows, n)]
        swap = send(mine((1, 0, rows)), place(s, (1, 0, rows)), dev_c1, "c1", kib((1, 0, rows)))
        first = far_piece(pieces[0], False)
        local.start()
        across(s, (0, 0, rows), mine((0, 0, rows)), False)
        plan.spawn(swapped())
        plan.spawn(later(pieces[1:], first))

    def scaled(r0, nr, block):
        column = pl.multiple_of(block * 256, 256)
        row_gain = gain[:, pl.ds(pl.multiple_of(block * 512 + kappa * 256, 256), 256)]
        fresh = r0 not in begun
        begun.add(r0)

        @pl.loop(0, nr // 16)
        def _(i):
            rows = pl.ds(pl.multiple_of(r0 + i * 16, 16), 16)
            x = xr[block, rows, :].astype(F32)
            total = x[:, :128] * x[:, :128] + x[:, 128:] * x[:, 128:]
            xn[rows, pl.ds(column, 256)] = (x * row_gain).astype(BF16)
            ssq[rows, :] = total if fresh else ssq[rows, :] + total

        plan.busy(nr / 900)

    begun = set()

    def squares(chunk):
        r0, r1 = CHUNKS[chunk]
        ssend[chunk, :, 0 : r1 - r0] = lax.dot_general(
            jnp.ones((8, 128), F32), ssq[r0:r1, :], (((1,), (1,)), ((), ())),
            precision=lax.Precision.HIGHEST, preferred_element_type=F32,
        )
        plan.busy(0.2)

    def product(chunk, half):
        r0, r1 = CHUNKS[chunk]
        cols = slice(half * 384, half * 384 + 384)
        acc[r0:r1, :] = jnp.dot(xn[r0:r1, 0:1024], panel[0:1024, cols], preferred_element_type=F32)

        @pl.loop(1, 4)
        def _(k):
            depth = pl.ds(pl.multiple_of(k * 1024, 1024), 1024)
            acc[r0:r1, :] += jnp.dot(xn[r0:r1, depth], panel[depth, cols], preferred_element_type=F32)

        plan.busy(0.4 + (r1 - r0) / 320)

    def combine(chunk):
        r0, r1 = CHUNKS[chunk]
        nr = r1 - r0
        both = ssend[chunk, :, 0:nr] + srecv[chunk, :, 0:nr]
        eye = (lax.broadcasted_iota(jnp.int32, (nr, nr), 0) == lax.broadcasted_iota(jnp.int32, (nr, nr), 1)).astype(F32)
        column = lax.dot_general(
            eye, both, (((1,), (1,)), ((), ())), precision=lax.Precision.HIGHEST, preferred_element_type=F32
        )[:, 0:1]
        scale = lax.rsqrt(column * (1.0 / 8192.0) + 1e-06)
        total = acc[r0:r1, :] + precv[r0:r1, :].astype(F32)
        feats[r0 + HALO : r1 + HALO, :] = total * scale
        plan.busy(nr / 250)

    def gated_rows(chunk):
        r0, r1 = CHUNKS[chunk]
        return (r0 + 16 if r0 else 0), (r1 + 16 if chunk else SLAB)

    def gates(chunk):
        t0, t1 = gated_rows(chunk)
        nr, e0 = t1 - t0, t0 + HALO

        def filtered(i, begin, rows):
            value = jnp.zeros((rows, 128), F32)
            for lag in range(3):
                value = value + pre[lag, i : i + 1, :] * feats[begin - lag : begin - lag + rows, i * 128 : i * 128 + 128]
            return value

        kv[e0 - 8 : e0 + nr, :] = filtered(1, e0 - 8, nr + 8) * filtered(2, e0 - 8, nr + 8)
        value = jnp.zeros((nr, 128), F32)
        for lag in range(7):
            value = value + inner[lag : lag + 1, :] * kv[e0 - lag : e0 - lag + nr, :]
        block = pl.multiple_of((2 * z + high) * 128, 128)
        gat[t0:t1, pl.ds(block, 128)] = (filtered(0, e0, nr) * value).astype(BF16)
        plan.busy(nr / 200)

    def product_out(chunk, half):
        t0, t1 = gated_rows(chunk)
        cols = slice(half * 256, half * 256 + 256)
        plan.busy(0.3 + (t1 - t0) / 600)
        return jnp.dot(gat[t0:t1, :], panel_out[:, cols], preferred_element_type=F32)

    def x_view(r0, r1):
        return lambda block: xr.at[block, pl.ds(r0, r1 - r0), :]

    def g_view(t0, t1):
        return lambda block: gat.at[pl.ds(t0, t1 - t0), pl.ds(pl.multiple_of(block * 128, 128), 128)]

    halo, stores = [], []

    def tokens_of(i):
        r0, r1 = TOKEN_ROWS[i]
        if i:
            yield [TOKEN_BEGIN[i]]
        gather(
            x_view(r0, r1), (r1 - r0) / 2, lambda block: scaled(r0, r1 - r0, block), f"x{r0}", TREES[TOKEN_TREE[i]]
        )
        yield [0.0]

    def compute(chunk):
        r0, r1 = CHUNKS[chunk]
        t0, t1 = gated_rows(chunk)
        yield [f"x{a}" for a, b in TOKEN_ROWS if r0 <= a < r1]
        squares(chunk)
        k2 = send(ssend.at[chunk], srecv.at[chunk], dev_c1, "c1", 12)
        yield ["w"]
        product(chunk, 1)
        psend[r0:r1, :] = acc[r0:r1, :].astype(BF16)
        k1 = send(psend.at[pl.ds(r0, r1 - r0), :], precv.at[pl.ds(r0, r1 - r0), :], dev_c1, "c1", (r1 - r0) * 0.75)
        yield [0.0]
        product(chunk, 0)
        yield [k1, k2] + [f"f{i}" for i in range(chunk)]
        arrived(k2, srecv.at[chunk])
        arrived(k1, precv.at[pl.ds(r0, r1 - r0), :])
        combine(chunk)
        plan.flags.add(f"f{chunk}")
        if chunk == 0:
            halo.append(send(feats.at[pl.ds(EXT - 8, 8), :], edge, dev_next, "c1", 12))
        if r0 == 0:
            yield [halo[0]]
            arrived(halo[0], edge)
            feats[8:16, :] = jnp.where(s == 0, 0.0, edge[...])
        gates(chunk)
        gather(g_view(t0, t1), (t1 - t0) / 4, lambda block: None, f"g{chunk}", TREES[GATED_TREE[chunk]])
        yield [f"g{chunk}", "wo"]
        osend[t0:t1, :] = product_out(chunk, 1).astype(BF16)
        k3 = send(osend.at[pl.ds(t0, t1 - t0), :], orecv.at[pl.ds(t0, t1 - t0), :], dev_c1, "c1", (t1 - t0) / 2)
        yield [0.0]
        acc2[t0:t1, :] = product_out(chunk, 0)
        yield [k3]
        arrived(k3, orecv.at[pl.ds(t0, t1 - t0), :])
        out[t0:t1, :] = (acc2[t0:t1, :] + orecv[t0:t1, :].astype(F32)).astype(BF16)
        store = pltpu.make_async_copy(out.at[pl.ds(t0, t1 - t0), :], out_hbm.at[pl.ds(t0, t1 - t0), :], store_sem.at[chunk])
        store.start()
        stores.append(store)
        plan.busy((t1 - t0) / 1000)

    def out_weights():
        yield [WO_BEGIN]
        weights(wo, panel_out, 128, 256, "wo", local_sem.at[1])

    plan.spawn(tokens_of(0))
    weights(wf, panel, 256, 384, "w", local_sem.at[0])
    for i in range(1, len(TOKEN_ROWS)):
        plan.spawn(tokens_of(i))
    plan.spawn(out_weights())
    for chunk in range(len(CHUNKS)):
        plan.spawn(compute(chunk), 2 + chunk)
    plan.run()
    for store in stores:
        store.wait()
    for k in range(len(started)):
        sent(k)
    assert len(started) <= N_RECV, len(started)


def on_device(tokens, norm_gain, w_feat, pre_taps, inner_taps, w_out):
    hbm = pl.BlockSpec(memory_space=pl.ANY)
    return pl.pallas_call(
        body,
        out_shape=jax.ShapeDtypeStruct((SLAB, 256), BF16),
        in_specs=[hbm] * 6,
        out_specs=hbm,
        scratch_shapes=[
            pltpu.VMEM((1, 8192), F32),
            pltpu.VMEM((3, 3, 128), F32),
            pltpu.VMEM((7, 128), F32),
            pltpu.VMEM((256, 256), BF16),
            pltpu.VMEM((SLAB, 256), BF16),
            pltpu.VMEM((SLAB, 384), BF16),
            pltpu.VMEM((16, SLAB, 256), BF16),
            pltpu.VMEM((SLAB, 4096), BF16),
            pltpu.VMEM((4096, 768), BF16),
            pltpu.VMEM((2048, 512), BF16),
            pltpu.VMEM((SLAB, 384), F32),
            pltpu.VMEM((SLAB, 384), BF16),
            pltpu.VMEM((SLAB, 384), BF16),
            pltpu.VMEM((EXT, 384), F32),
            pltpu.VMEM((8, 384), F32),
            pltpu.VMEM((EXT, 128), F32),
            pltpu.VMEM((SLAB, 128), F32),
            pltpu.VMEM((len(CHUNKS), 8, 384), F32),
            pltpu.VMEM((len(CHUNKS), 8, 384), F32),
            pltpu.VMEM((SLAB, 2048), BF16),
            pltpu.VMEM((SLAB, 256), F32),
            pltpu.VMEM((SLAB, 256), BF16),
            pltpu.VMEM((SLAB, 256), BF16),
            pltpu.SemaphoreType.DMA((N_SEND,)),
            pltpu.SemaphoreType.DMA((N_RECV,)),
            pltpu.SemaphoreType.DMA((2,)),
            pltpu.SemaphoreType.DMA((8,)),
            pltpu.SemaphoreType.DMA((len(CHUNKS),)),
        ],
        compiler_params=pltpu.CompilerParams(
            collective_id=0, has_side_effects=True, vmem_limit_bytes=56 * 1024 * 1024
        ),
    )(
        tokens,
        norm_gain.reshape(1, 8192),
        jnp.moveaxis(w_feat, 1, 0),
        pre_taps,
        inner_taps,
        w_out,
    )


def solution(mesh):
    in_specs = (
        P("seq", ("fsdp", "chan")),
        P(),
        P("seq", None, ("fsdp", "chan")),
        P(None, None, ("fsdp", "chan")),
        P(None, ("fsdp", "chan")),
        P("seq", ("fsdp", "chan")),
    )
    out_specs = P("seq", ("fsdp", "chan"))
    return jax.shard_map(
        on_device, mesh=mesh, in_specs=in_specs, out_specs=out_specs, check_vma=False
    )
```

```python
import jax
import jax.numpy as jnp
from jax import lax
from jax.experimental import pallas as pl
from jax.experimental.pallas import tpu as pltpu
from jax.sharding import PartitionSpec as P

MESH = pl.DeviceIdType.MESH
F32, BF16 = jnp.float32, jnp.bfloat16
SLAB, HALO, EXT = 512, 16, 528
N_SEND, N_RECV = 40, 211
TOKEN_ROWS = ((384, 512), (256, 384), (128, 256), (0, 128))
CHUNKS = ((384, 512), (256, 384), (128, 256), (0, 128))
RATE = {"z+": 45.0, "z-": 45.0, "x+": 45.0, "x-": 45.0, "y": 22.5, "c1": 45.0, "core": 400.0}
LATENCY = {"z+": 2.8, "z-": 2.8, "x+": 2.8, "x-": 2.8, "y": 2.8, "c1": 2.8, "core": 2.8}
FAIR = ("y", "c1")
TOKEN_BEGIN = (0.0, 1.6, 5.3, 26.8)
TOKEN_TURN = (0.0, 0.0, 0.0, 0.0)
RIGHT, LEFT = {(1, 0): [(2, 0)], (2, 0): [(3, 0)], (3, 0): [(4, 0)]}, {(-1, 0): [(-2, 0)], (-2, 0): [(-3, 0)]}
OTHER = {(1, 1): [(2, 1)], (2, 1): [(3, 1)], (-1, 1): [(-2, 1)], (-2, 1): [(-3, 1)], (-3, 1): [(-4, 1)]}
SKIP = {
    (1, 0): [(3, 0), (2, 0)], (3, 0): [(4, 0)], (-1, 0): [(-2, 0)], (-2, 0): [(-3, 0)],
    (1, 1): [(2, 1)], (2, 1): [(3, 1)], (-1, 1): [(-3, 1), (-2, 1)], (-3, 1): [(-4, 1)],
}
OTHER_Y = {(1, 1): [(2, 1)], (2, 1): [(3, 1)], (-1, 1): [(-2, 1)], (-2, 1): [(-3, 1)], (4, 0): [(4, 1)]}
TREES = {
    "ring": {(0, 0): [(0, 1), (1, 0), (-1, 0)], (0, 1): [(-1, 1), (1, 1)], **RIGHT, **LEFT, **OTHER},
    "diag": {(0, 0): [(1, 0), (-1, 0), (-1, 1), (1, 1), (0, 1)], **RIGHT, **LEFT, **OTHER},
    "skip": {(0, 0): [(0, 1), (1, 0), (-1, 0)], (0, 1): [(-1, 1), (1, 1)], **SKIP},
    "fast": {(0, 0): [(1, 0), (-1, 1), (-1, 0), (1, 1), (0, 1)], **SKIP},
    "ydia": {
        (0, 0): [(1, 0), (-1, 0), (-1, 1), (1, 1), (0, 1)], **RIGHT, **LEFT, **OTHER_Y,
    },
    "late": {(0, 0): [(1, 0), (-1, 0), (0, 1)], (0, 1): [(-1, 1), (1, 1)], **RIGHT, **LEFT, **OTHER},
    "viay": {(0, 0): [(0, 1), (1, 0), (-1, 0)], (0, 1): [(-1, 1), (1, 1)], **RIGHT, **LEFT, **OTHER_Y},
}
TREES["all"] = {(0, 0): [(d, side) for d in (4, 1, -1, 2, -2, 3, -3) for side in (0, 1)] + [(0, 1)]}
TREES["half"] = {(0, 0): [(0, 1)] + [(d, 0) for d in (4, 1, -1, 2, -2, 3, -3)], (0, 1): [(d, 1) for d in (-4, 1, -1, 2, -2, 3, -3)]}
TREES["duo"] = {
    (0, 0): [(0, 1), (2, 0), (-2, 0), (1, 0), (-1, 0)], (2, 0): [(4, 0), (3, 0)], (-2, 0): [(-3, 0)],
    (0, 1): [(-2, 1), (2, 1), (1, 1), (-1, 1)], (-2, 1): [(-4, 1), (-3, 1)], (2, 1): [(3, 1)],
}
TOKEN_TREE = ("ring", "viay", "ring", "skip")
GATED_TREE = ("ring", "diag", "viay", "fast")
WO_BEGIN = 33.0
FAR_AFTER = True
W_FIRST = False
LEAF_SLACK = 1.5
WO_SPLIT = 1
FAR_SPLIT = 2
FAR_DIRECT = True


class Plan:
    def __init__(self):
        self.clock, self.flows, self.landed, self.left = 0.0, [], {}, {}
        self.flags, self.streams, self.order, self.log = set(), [], 0, []

    def spawn(self, gen, rank=0):
        self.order += 1
        self.resume([rank, self.order, gen, None])

    def resume(self, stream):
        stream[3] = next(stream[2], None)
        if stream[3] is not None:
            self.streams.append(stream)

    def start(self, key, link, kib):
        if key is None:
            self.order += 1
            key = -self.order
        self.flows.append([key, link, float(kib)])
        self.clock_to(self.clock + 0.12)

    def busy(self, us):
        self.clock_to(self.clock + us)

    def shares(self):
        total = {}
        for flow in self.flows:
            total.setdefault(flow[1], []).append(flow)
        share = {}
        for link, flows in total.items():
            for i, flow in enumerate(flows):
                share[flow[0]] = RATE[link] / len(flows) if link in FAIR else RATE[link] * (i == 0)
        return share

    def clock_to(self, until):
        while True:
            share = self.shares()
            ends = [flow[2] / share[flow[0]] for flow in self.flows if share[flow[0]]]
            step = min(ends + [until - self.clock])
            for flow in self.flows:
                flow[2] -= step * share[flow[0]]
            self.clock += step
            for flow in [f for f in self.flows if f[2] <= 1e-6]:
                self.flows.remove(flow)
                self.left[flow[0]] = self.clock + 0.3
                self.landed[flow[0]] = self.clock + LATENCY[flow[1]]
            if self.clock >= until - 1e-9:
                return

    def when(self, need):
        if isinstance(need, float):
            return need
        if isinstance(need, str):
            return 0.0 if need in self.flags else None
        if isinstance(need, tuple):
            times, more = (self.left, 0.0) if need[0] == "sent" else (self.landed, LEAF_SLACK)
            return times[need[1]] + more if need[1] in times else None
        return self.landed.get(need)

    def run(self):
        while self.streams:
            best = None
            for stream in self.streams:
                times = [self.when(need) for need in stream[3]]
                if any(t is None for t in times):
                    continue
                at = max(times + [0.0])
                ready = (max(at, self.clock), stream[0], at, stream[1])
                if best is None or ready < best[0]:
                    best = (ready, stream)
            share = self.shares()
            ends = [self.clock + flow[2] / share[flow[0]] for flow in self.flows if share[flow[0]]]
            if best is not None and (not ends or best[0][0] <= min(ends)):
                self.clock_to(max(best[0][0], self.clock))
                self.streams.remove(best[1])
                self.resume(best[1])
            else:
                self.clock_to(min(ends))


def body(
    tok_hbm, gain_hbm, w3, pre_hbm, inner_hbm, wo_hbm, out_hbm,
    gain, pre, inner, wo, out, wf, xr, xn, panel, panel_out, acc, psend, precv, feats, edge, kv, ssq, ssend, srecv, gat, acc2, osend, orecv,
    send_sem, recv_sem, local_sem, load_sem, store_sem,
):
    s, z, c = lax.axis_index("seq"), lax.axis_index("fsdp"), lax.axis_index("chan")
    kappa = lax.rem(c, 2)
    high = c // 2
    c1 = c + 1 - 2 * kappa
    c2 = lax.rem(c + 2, 4)
    core = lax.rem(s, 2)
    y_hi = lax.rem(s // 2, 2)
    s_yh = s + 2 - 4 * y_hi
    s_sib = s + 1 - 2 * core
    zp, zm = (s, lax.rem(z + 1, 8), c), (s, lax.rem(z + 7, 8), c)
    dev_c1, dev_c2 = (s, z, c1), (s, z, c2)
    dev_yh, dev_yh1 = (s_yh, z, c), (s_yh, z, c1)
    xp, xm = (lax.rem(s + 4, 16), z, c), (lax.rem(s + 12, 16), z, c)
    xf = (lax.rem(s + 8, 16), z, c)
    dev_sib = (s_sib, z, c)
    dev_next, dev_prev = (lax.rem(s + 1, 16), z, c), (lax.rem(s + 15, 16), z, c)
    peers = (zp, zm, dev_c1, dev_c2, dev_yh, dev_yh1, xp, xm, xf, dev_sib, dev_next, dev_prev)

    barrier = pltpu.get_barrier_semaphore()
    for dev in peers:
        pl.semaphore_signal(barrier, inc=1, device_id=dev, device_id_type=MESH)
    loads = [
        pltpu.make_async_copy(src, dst, load_sem.at[i])
        for i, (src, dst) in enumerate(
            [(tok_hbm, xr.at[2 * z + high])]
            + [(w3.at[i], wf.at[:, pl.ds(i * 128, 128)]) for i in range(3)]
            + [(wo_hbm, wo), (gain_hbm, gain), (pre_hbm, pre), (inner_hbm, inner)]
        )
    ]
    for load in loads:
        load.start()
    feats[0:8, :] = jnp.zeros((8, 384), F32)
    ssend[...] = jnp.zeros_like(ssend)
    pl.semaphore_wait(barrier, len(peers))
    for load in loads:
        load.wait()

    plan = Plan()
    started, flying = [], []

    def send(src, dst, dev, link, kib):
        k = len(started)
        if len(flying) < N_SEND:
            slot = len(flying)
        else:
            old, slot = flying.pop(0)
            sent(old)
        copy = pltpu.make_async_remote_copy(src, dst, send_sem.at[slot], recv_sem.at[k], device_id=dev, device_id_type=MESH)
        copy.start()
        started.append([copy, False])
        flying.append((k, slot))
        plan.start(k, link, kib)
        return k

    def sent(k):
        if not started[k][1]:
            started[k][0].wait_send()
            started[k][1] = True

    def arrived(k, landed):
        pltpu.make_async_remote_copy(
            landed, landed, send_sem.at[0], recv_sem.at[k], device_id=zp, device_id_type=MESH
        ).wait_recv()

    def block_of(steps, hi):
        return 2 * lax.rem(z + steps + 8, 8) + hi

    def gather(view, kib, use, flag, tree, turn_at=0.0):
        count = [0]

        def holder(node):
            return block_of(-node[0], high if node[1] == 0 else 1 - high)

        def hand(node, child):
            steps, turn = child[0] - node[0], child[1] != node[1]
            dev = (s, lax.rem(z + steps + 8, 8), c2 if turn else c)
            link = "z+" if steps > 0 else "z-"
            if turn and steps:
                plan.start(None, link, kib)
            ref = view(holder(node))
            k = send(ref, ref, dev, "y" if turn else link, kib * (1 if turn else abs(steps)))
            plan.spawn(take(child, k))

        def turn_later(child):
            yield [turn_at]
            hand((0, 0), child)

        def pass_on(node):
            for child in tree.get(node, ()):
                if turn_at and node == (0, 0) and child[1]:
                    plan.spawn(turn_later(child))
                else:
                    hand(node, child)
            use(holder(node))
            count[0] += 1
            if count[0] == 16:
                plan.flags.add(flag)

        def take(node, k):
            yield [k if node in tree else ("leaf", k)]
            arrived(k, view(holder(node)))
            pass_on(node)

        pass_on((0, 0))

    def weights(src, dst, rows, cols, key, sem):
        def place(block, piece):
            part, r0, nr = piece
            return dst.at[pl.ds(pl.multiple_of(block * rows + r0, 16), nr), pl.ds(part * cols, cols)]

        def mine(piece):
            part, r0, nr = piece
            half = kappa if part == 0 else 1 - kappa
            return src.at[pl.ds(pl.multiple_of(half * rows + r0, 16), nr), :]

        def kib(piece):
            return piece[2] * cols * 2 / 1024

        rest, sib = [16 * rows], []
        local = pltpu.make_async_copy(mine((0, 0, rows)), place(s, (0, 0, rows)), sem)

        def to_sibling(base, far, piece, ref):
            k = send(ref, place(lax.rem(base + far, 16), piece), dev_sib, "core", kib(piece))
            sib.append((k, place(lax.rem(base + 1 - 2 * core + far, 16), piece)))
            rest[0] -= piece[2]
            if not rest[0]:
                plan.spawn(finish(), 1)

        def finish():
            yield [k for k, _ in sib]
            for k, ref in sib:
                arrived(k, ref)
            local.wait()
            plan.flags.add(key)

        def across(base, piece, ref, direct):
            part = piece[0]
            kr = send(ref, place(base, piece), xp, "x+", kib(piece))
            kl = send(ref, place(base, piece), xm, "x-", kib(piece))
            if direct:
                plan.start(None, "x-", kib(piece))
                kf = send(ref, place(base, piece), xf, "x+", kib(piece))

            def take(k, far, onward, dev, link):
                yield [k]
                ref = place(lax.rem(base + far, 16), piece)
                arrived(k, ref)
                if onward:
                    k = send(ref, ref, dev, link, kib(piece))
                to_sibling(base, far, piece, ref)
                if onward:
                    yield [k]
                    ref = place(lax.rem(base + 8, 16), piece)
                    arrived(k, ref)
                    to_sibling(base, 8, piece, ref)

            plan.spawn(take(kr, 12, part == 0 and not direct, xp, "x+"))
            plan.spawn(take(kl, 4, part == 1 and not direct, xm, "x-"))
            if direct:
                plan.spawn(take(kf, 8, False, None, None))
            to_sibling(base, 0, piece, ref)

        def far(k, piece, direct):
            yield [k]
            arrived(k, place(s_yh, piece))
            across(s_yh, piece, place(s_yh, piece), direct)

        def far_piece(piece, direct):
            k = send(mine(piece), place(s, piece), dev_yh if piece[0] == 0 else dev_yh1, "y", kib(piece))
            plan.spawn(far(k, piece, direct))
            return k

        def swapped():
            yield [swap]
            arrived(swap, place(s, (1, 0, rows)))
            across(s, (1, 0, rows), place(s, (1, 0, rows)), False)

        def later(pieces, k):
            for i, piece in enumerate(pieces):
                if FAR_AFTER:
                    yield [("sent", k)]
                    sent(k)
                k = far_piece(piece, FAR_DIRECT and i == len(pieces) - 1)
            yield [0.0]

        n = rows // (FAR_SPLIT if key == "w" else WO_SPLIT)
        pieces = [(part, r0, n) for part in (0, 1) for r0 in range(0, rows, n)]
        swap = send(mine((1, 0, rows)), place(s, (1, 0, rows)), dev_c1, "c1", kib((1, 0, rows)))
        first = far_piece(pieces[0], False)
        local.start()
        across(s, (0, 0, rows), mine((0, 0, rows)), False)
        plan.spawn(swapped())
        plan.spawn(later(pieces[1:], first))

    def scaled(r0, nr, block):
        column = pl.multiple_of(block * 256, 256)
        row_gain = gain[:, pl.ds(pl.multiple_of(block * 512 + kappa * 256, 256), 256)]
        fresh = r0 not in begun
        begun.add(r0)

        @pl.loop(0, nr // 16)
        def _(i):
            rows = pl.ds(pl.multiple_of(r0 + i * 16, 16), 16)
            x = xr[block, rows, :].astype(F32)
            total = x[:, :128] * x[:, :128] + x[:, 128:] * x[:, 128:]
            xn[rows, pl.ds(column, 256)] = (x * row_gain).astype(BF16)
            ssq[rows, :] = total if fresh else ssq[rows, :] + total

        plan.busy(nr / 2500)

    begun = set()

    def squares(chunk):
        r0, r1 = CHUNKS[chunk]
        ssend[chunk, :, 0 : r1 - r0] = lax.dot_general(
            jnp.ones((8, 128), F32), ssq[r0:r1, :], (((1,), (1,)), ((), ())),
            precision=lax.Precision.HIGHEST, preferred_element_type=F32,
        )
        plan.busy(0.3)

    def product(chunk, half):
        r0, r1 = CHUNKS[chunk]
        cols = slice(half * 384, half * 384 + 384)
        acc[r0:r1, :] = jnp.dot(xn[r0:r1, :], panel[:, cols], preferred_element_type=F32)

        plan.busy(0.35 + (r1 - r0) / 200)

    def combine(chunk):
        r0, r1 = CHUNKS[chunk]
        nr = r1 - r0
        both = ssend[chunk, :, 0:nr] + srecv[chunk, :, 0:nr]
        eye = (lax.broadcasted_iota(jnp.int32, (nr, nr), 0) == lax.broadcasted_iota(jnp.int32, (nr, nr), 1)).astype(F32)
        column = lax.dot_general(
            eye, both, (((1,), (1,)), ((), ())), precision=lax.Precision.HIGHEST, preferred_element_type=F32
        )[:, 0:1]
        scale = lax.rsqrt(column * (1.0 / 8192.0) + 1e-06)
        total = acc[r0:r1, :] + precv[r0:r1, :].astype(F32)
        feats[r0 + HALO : r1 + HALO, :] = total * scale
        plan.busy(0.1 + nr / 2000)

    def gated_rows(chunk):
        r0, r1 = CHUNKS[chunk]
        return (r0 + 16 if r0 else 0), (r1 + 16 if chunk else SLAB)

    def gates(chunk):
        t0, t1 = gated_rows(chunk)
        nr, e0 = t1 - t0, t0 + HALO

        def filtered(i, begin, rows):
            value = jnp.zeros((rows, 128), F32)
            for lag in range(3):
                value = value + pre[lag, i : i + 1, :] * feats[begin - lag : begin - lag + rows, i * 128 : i * 128 + 128]
            return value

        kv[e0 - 8 : e0 + nr, :] = filtered(1, e0 - 8, nr + 8) * filtered(2, e0 - 8, nr + 8)
        value = jnp.zeros((nr, 128), F32)
        for lag in range(7):
            value = value + inner[lag : lag + 1, :] * kv[e0 - lag : e0 - lag + nr, :]
        block = pl.multiple_of((2 * z + high) * 128, 128)
        gat[t0:t1, pl.ds(block, 128)] = (filtered(0, e0, nr) * value).astype(BF16)
        plan.busy(0.05 + nr / 3000)

    def product_out(chunk, half):
        t0, t1 = gated_rows(chunk)
        cols = slice(half * 256, half * 256 + 256)
        plan.busy(0.1 + (t1 - t0) / 2000)
        return jnp.dot(gat[t0:t1, :], panel_out[:, cols], preferred_element_type=F32)

    def x_view(r0, r1):
        return lambda block: xr.at[block, pl.ds(r0, r1 - r0), :]

    def g_view(t0, t1):
        return lambda block: gat.at[pl.ds(t0, t1 - t0), pl.ds(pl.multiple_of(block * 128, 128), 128)]

    halo, stores = [], []

    def tokens_of(i):
        r0, r1 = TOKEN_ROWS[i]
        if TOKEN_BEGIN[i]:
            yield [TOKEN_BEGIN[i]]
        gather(
            x_view(r0, r1), (r1 - r0) / 2, lambda block: scaled(r0, r1 - r0, block), f"x{r0}", TREES[TOKEN_TREE[i]], TOKEN_TURN[i]
        )
        yield [0.0]

    def compute(chunk):
        r0, r1 = CHUNKS[chunk]
        t0, t1 = gated_rows(chunk)
        yield [f"x{a}" for a, b in TOKEN_ROWS if r0 <= a < r1]
        squares(chunk)
        k2 = send(ssend.at[chunk], srecv.at[chunk], dev_c1, "c1", 12)
        yield ["w"]
        product(chunk, 1)
        psend[r0:r1, :] = acc[r0:r1, :].astype(BF16)
        k1 = send(psend.at[pl.ds(r0, r1 - r0), :], precv.at[pl.ds(r0, r1 - r0), :], dev_c1, "c1", (r1 - r0) * 0.75)
        yield [0.0]
        product(chunk, 0)
        yield [k1, k2] + [f"f{i}" for i in range(chunk)]
        arrived(k2, srecv.at[chunk])
        arrived(k1, precv.at[pl.ds(r0, r1 - r0), :])
        combine(chunk)
        plan.flags.add(f"f{chunk}")
        if chunk == 0:
            halo.append(send(feats.at[pl.ds(EXT - 8, 8), :], edge, dev_next, "c1", 12))
        if r0 == 0:
            yield [halo[0]]
            arrived(halo[0], edge)
            feats[8:16, :] = jnp.where(s == 0, 0.0, edge[...])
        gates(chunk)
        gather(g_view(t0, t1), (t1 - t0) / 4, lambda block: None, f"g{chunk}", TREES[GATED_TREE[chunk]])
        yield [f"g{chunk}", "wo"]
        osend[t0:t1, :] = product_out(chunk, 1).astype(BF16)
        k3 = send(osend.at[pl.ds(t0, t1 - t0), :], orecv.at[pl.ds(t0, t1 - t0), :], dev_c1, "c1", (t1 - t0) / 2)
        yield [0.0]
        acc2[t0:t1, :] = product_out(chunk, 0)
        yield [k3]
        arrived(k3, orecv.at[pl.ds(t0, t1 - t0), :])
        out[t0:t1, :] = (acc2[t0:t1, :] + orecv[t0:t1, :].astype(F32)).astype(BF16)
        store = pltpu.make_async_copy(out.at[pl.ds(t0, t1 - t0), :], out_hbm.at[pl.ds(t0, t1 - t0), :], store_sem.at[chunk])
        store.start()
        stores.append(store)
        plan.busy((t1 - t0) / 1000)

    def out_weights():
        yield [WO_BEGIN]
        weights(wo, panel_out, 128, 256, "wo", local_sem.at[1])

    if not W_FIRST:
        plan.spawn(tokens_of(0))
    weights(wf, panel, 256, 384, "w", local_sem.at[0])
    if W_FIRST:
        plan.spawn(tokens_of(0))
    for i in range(1, len(TOKEN_ROWS)):
        plan.spawn(tokens_of(i))
    plan.spawn(out_weights())
    for chunk in range(len(CHUNKS)):
        plan.spawn(compute(chunk), 2 + chunk)
    plan.run()
    for store in stores:
        store.wait()
    for k in range(len(started)):
        sent(k)
    assert len(started) <= N_RECV, len(started)


def on_device(tokens, norm_gain, w_feat, pre_taps, inner_taps, w_out):
    hbm = pl.BlockSpec(memory_space=pl.ANY)
    return pl.pallas_call(
        body,
        out_shape=jax.ShapeDtypeStruct((SLAB, 256), BF16),
        in_specs=[hbm] * 6,
        out_specs=hbm,
        scratch_shapes=[
            pltpu.VMEM((1, 8192), F32),
            pltpu.VMEM((3, 3, 128), F32),
            pltpu.VMEM((7, 128), F32),
            pltpu.VMEM((256, 256), BF16),
            pltpu.VMEM((SLAB, 256), BF16),
            pltpu.VMEM((SLAB, 384), BF16),
            pltpu.VMEM((16, SLAB, 256), BF16),
            pltpu.VMEM((SLAB, 4096), BF16),
            pltpu.VMEM((4096, 768), BF16),
            pltpu.VMEM((2048, 512), BF16),
            pltpu.VMEM((SLAB, 384), F32),
            pltpu.VMEM((SLAB, 384), BF16),
            pltpu.VMEM((SLAB, 384), BF16),
            pltpu.VMEM((EXT, 384), F32),
            pltpu.VMEM((8, 384), F32),
            pltpu.VMEM((EXT, 128), F32),
            pltpu.VMEM((SLAB, 128), F32),
            pltpu.VMEM((len(CHUNKS), 8, 384), F32),
            pltpu.VMEM((len(CHUNKS), 8, 384), F32),
            pltpu.VMEM((SLAB, 2048), BF16),
            pltpu.VMEM((SLAB, 256), F32),
            pltpu.VMEM((SLAB, 256), BF16),
            pltpu.VMEM((SLAB, 256), BF16),
            pltpu.SemaphoreType.DMA((N_SEND,)),
            pltpu.SemaphoreType.DMA((N_RECV,)),
            pltpu.SemaphoreType.DMA((2,)),
            pltpu.SemaphoreType.DMA((8,)),
            pltpu.SemaphoreType.DMA((len(CHUNKS),)),
        ],
        compiler_params=pltpu.CompilerParams(
            collective_id=0, has_side_effects=True, vmem_limit_bytes=56 * 1024 * 1024
        ),
    )(
        tokens,
        norm_gain.reshape(1, 8192),
        jnp.moveaxis(w_feat, 1, 0),
        pre_taps,
        inner_taps,
        w_out,
    )


def solution(mesh):
    in_specs = (
        P("seq", ("fsdp", "chan")),
        P(),
        P("seq", None, ("fsdp", "chan")),
        P(None, None, ("fsdp", "chan")),
        P(None, ("fsdp", "chan")),
        P("seq", ("fsdp", "chan")),
    )
    out_specs = P("seq", ("fsdp", "chan"))
    return jax.shard_map(
        on_device, mesh=mesh, in_specs=in_specs, out_specs=out_specs, check_vma=False
    )
```
